256 devices in a mesh: gy: 8 (over z), gx: 32 (over y, x, core).
Axes of the slice: x: 4, y: 4, z: 8, core: 2. Of those that a mesh axis runs over, the one named last changes fastest.
Arguments:
- increment: float32 [64, 64, 4096], P(None, 'gy', 'gx'), may hold values from -6 to 6
- residual: float32 [64, 64, 4096], P(None, 'gy', 'gx'), as said below
- direction: float32 [64, 64, 4096], P(None, 'gy', 'gx'), as said below
- wind_east: float32 [64, 64, 4096], P(None, 'gy', 'gx'), may hold values from -4 to 4
- wind_north: float32 [64, 64, 4096], P(None, 'gy', 'gx'), may hold values from -4 to 4
- obs_column: int32 [4, 1048576], P(None, ('gy', 'gx')), may hold values from 0 to 1023
- obs_count: int32 [4, 8192], P(None, ('gy', 'gx')), may hold values from 1 to 128, as said below
- obs_weight: float32 [4, 64, 1048576], P(None, None, ('gy', 'gx')), may hold values from 0.25 to 4
Outputs:
- new_increment: float32 [64, 64, 4096], P(None, 'gy', 'gx')
- new_residual: float32 [64, 64, 4096], P(None, 'gy', 'gx')
- new_direction: float32 [64, 64, 4096], P(None, 'gy', 'gx')
The draws below stay inside these ranges and needn't reach their ends.
Inputs may be any that keep to these rules, and one draw needn't show every extreme that they name: `obs_count`: slots at or past the count are ignored; at every step each owner fills all 128 slots for some grid device. `residual`: a real field. `direction`: a real field.
All inputs are finite; a program needn't handle non-finite values.
Results may differ from the reference program's by a relative error of at most 0.00016.
Values sent between devices are 32-bit elements; how exact they have to be, the bound alone decides.
A program may use at most 128 MiB of HBM per device.

```python
import math
import jax
import jax.numpy as jnp

L = 64
CY = 8
CX = 128
SLOT = 128
STEPS = 4
NY = 64
NX = 4096
NOBS = 1048576
N_GX = 32


def field_scale(key):
    row_key, col_key = jax.random.split(key)
    row_scale = 10.0 ** (0.5 * jax.random.uniform(row_key, (NY,), jnp.float32))
    col_ramp = 1.0 + 2.0 * jnp.arange(NX, dtype=jnp.float32) / max(NX - 1, 1)
    col_scale = 10.0 ** (0.5 * jax.random.uniform(col_key, (NX,), jnp.float32)) * col_ramp
    return 0.2 * row_scale[:, None] * col_scale[None, :]


def draw_residual(key, part):
    key = jax.random.fold_in(key, 11)
    scale_key, value_key = jax.random.split(key)
    values = jax.random.truncated_normal(value_key, -4.0, 4.0, (L, NY, NX), jnp.float32)
    return values * field_scale(scale_key)[None]


def draw_direction(key, part):
    key = jax.random.fold_in(key, 12)
    scale_key, value_key = jax.random.split(key)
    values = jax.random.truncated_normal(value_key, -4.0, 4.0, (L, NY, NX), jnp.float32)
    return values * field_scale(scale_key)[None]


def draw_obs_count(key, part):
    key = jax.random.fold_in(key, 13)
    hot_key, rest_key = jax.random.split(key)
    owners = NX // CX
    row_groups = NY // CY
    hottest = jax.random.randint(hot_key, (STEPS, row_groups, 1, 1), 0, owners)
    target = jnp.arange(owners, dtype=jnp.int32)[None, None, None, :]
    others = jax.random.randint(rest_key, (STEPS, row_groups, owners, owners), 1, SLOT // 2 + 1)
    counts = jnp.where(target == hottest, SLOT, others)
    return counts.reshape(STEPS, row_groups * owners * owners).astype(jnp.int32)


def touch_ends(array, stream_key, low, largest):
    extent = array.shape
    index_at = [jax.random.randint(jax.random.fold_in(stream_key, axis), (), 0, extent[axis]) for axis in range(len(extent))]
    array = array.at[tuple(index_at)].set(low)
    longest = extent.index(max(extent))
    index_at[longest] = (index_at[longest] + 1) % extent[longest]
    return array.at[tuple(index_at)].set(largest)


def block_levels(key, extent, shards, smallest, high):
    def one(position, parts):
        heights = jax.random.uniform(jax.random.fold_in(jax.random.fold_in(key, 6), position), (parts,), jnp.float32, smallest / len(shards), high / len(shards))
        return jnp.repeat(jnp.exp(heights), extent[position] // parts).reshape((-1,) + (1,) * (len(extent) - position - 1))

    gain = one(*shards[0])
    for cut in shards[1:]:
        gain = gain * one(*cut)
    return gain


def normal_values(stream_key, extent, scale, limit, pieces=(), held_as=jnp.bfloat16):
    values = scale * jax.random.normal(stream_key, extent, jnp.float32)
    if pieces:
        values = values * block_levels(stream_key, extent, pieces, -0.22, 0.18)
    return jnp.clip(values, -limit, limit).astype(held_as)


def setup_inputs(seed: int = 0) -> dict:
    key_list = jax.random.split(jax.random.key(seed), 9)
    return {
        "increment": normal_values(key_list[0], (L, NY, NX), 1.0, 6.0, ((1, 8), (2, 32)), jnp.float32),
        "residual": draw_residual(jax.random.fold_in(key_list[8], 71), 0),
        "direction": draw_direction(jax.random.fold_in(key_list[8], 71), 0),
        "wind_east": normal_values(key_list[3], (L, NY, NX), 1.0, 4.0, ((1, 8), (2, 32)), jnp.float32),
        "wind_north": normal_values(key_list[4], (L, NY, NX), 1.0, 4.0, ((1, 8), (2, 32)), jnp.float32),
        "obs_column": touch_ends(jax.random.randint(key_list[5], (STEPS, NOBS), 0, CY * CX), jax.random.fold_in(key_list[5], 1), 0, (CY * CX) - 1).astype(jnp.int32),
        "obs_count": draw_obs_count(jax.random.fold_in(key_list[8], 71), 0),
        "obs_weight": jnp.clip(jnp.exp(math.log(4.0) - 2.7725887 * jax.random.uniform(key_list[7], (STEPS, L, NOBS), jnp.float32) ** block_levels(key_list[7], (STEPS, L, NOBS), ((2, 256),), -0.2, 0.2)), 0.25, 4.0),
    }


ADVECTION = 0.3
DIFFUSION = 0.1
MIXING = 0.1


def vertical_mix(field):
    upper = jnp.concatenate([field[1:], jnp.zeros_like(field[:1])], axis=0)
    lower = jnp.concatenate([jnp.zeros_like(field[:1]), field[:-1]], axis=0)
    return upper + lower - 2.0 * field


def tangent_step(field, wind_east, wind_north):
    padded = jnp.pad(field, ((0, 0), (1, 1), (1, 1)))
    east_diff = padded[:, 1:-1, 2:] - padded[:, 1:-1, :-2]
    north_diff = padded[:, 2:, 1:-1] - padded[:, :-2, 1:-1]
    beside_all = padded[:, 2:, 1:-1] + padded[:, :-2, 1:-1] + padded[:, 1:-1, 2:] + padded[:, 1:-1, :-2]
    return (field - ADVECTION * (wind_east * east_diff + wind_north * north_diff)
            + DIFFUSION * (beside_all - 4.0 * field) + MIXING * vertical_mix(field))


def adjoint_step(field, wind_east, wind_north):
    east_flux = jnp.pad(wind_east * field, ((0, 0), (1, 1), (1, 1)))
    north_flux = jnp.pad(wind_north * field, ((0, 0), (1, 1), (1, 1)))
    padded = jnp.pad(field, ((0, 0), (1, 1), (1, 1)))
    east_term = east_flux[:, 1:-1, 2:] - east_flux[:, 1:-1, :-2]
    north_term = north_flux[:, 2:, 1:-1] - north_flux[:, :-2, 1:-1]
    beside_all = padded[:, 2:, 1:-1] + padded[:, :-2, 1:-1] + padded[:, 1:-1, 2:] + padded[:, 1:-1, :-2]
    return (field + ADVECTION * (east_term + north_term)
            + DIFFUSION * (beside_all - 4.0 * field) + MIXING * vertical_mix(field))


def reference(increment, residual, direction, wind_east, wind_north, obs_column, obs_count, obs_weight):
    total = obs_column.shape[1]
    slot_ids = jnp.arange(total, dtype=jnp.int32)
    pair = slot_ids // SLOT
    slot = slot_ids % SLOT
    target = pair % N_GX
    row_group = pair // (N_GX * N_GX)
    live = slot[None, :] < jnp.take(obs_count, pair, axis=1)
    global_row = row_group[None, :] * CY + obs_column // CX
    global_col = target[None, :] * CX + obs_column % CX
    flat_index = (global_row * NX + global_col).astype(jnp.int32)
    current = direction
    forcings = []
    for moment in range(STEPS):
        current = tangent_step(current, wind_east, wind_north)
        flat_state = current.reshape(L, NY * NX)
        profile = jnp.take(flat_state, flat_index[moment], axis=1)
        live_weight = jnp.where(live[moment][None, :], obs_weight[moment], jnp.float32(0.0))
        weighted = profile * live_weight
        forcing = jnp.zeros((L, NY * NX), jnp.float32).at[:, flat_index[moment]].add(weighted)
        forcings.append(forcing.reshape(L, NY, NX))
    adjoint = forcings[STEPS - 1]
    for moment in range(STEPS - 2, -1, -1):
        adjoint = adjoint_step(adjoint, wind_east, wind_north) + forcings[moment]
    adjoint = adjoint_step(adjoint, wind_east, wind_north)
    hessian = direction + adjoint
    norm_now = jnp.sum(residual * residual)
    curvature = jnp.sum(direction * hessian)
    alpha = norm_now / curvature
    new_increment = increment + alpha * direction
    new_residual = residual - alpha * hessian
    norm_next = jnp.sum(new_residual * new_residual)
    new_direction = new_residual + (norm_next / norm_now) * direction
    return new_increment, new_residual, new_direction
```

```python
import functools

import jax
import jax.numpy as jnp
from jax import lax
from jax.experimental import pallas as pl
from jax.experimental.pallas import tpu as pltpu
from jax.sharding import PartitionSpec as P

MESH = pl.DeviceIdType.MESH
F32 = jnp.float32
STEPS = 4
L = 64
ROWS = 8
COLS = 128
CELLS = ROWS * COLS
PLANE = 32
DEPTH = 8
PITCH = 24
LEVELS = L + 2
GROUP = 4
CHUNKS = PLANE // GROUP
OPENING = 10
SENDS = STEPS * (PLANE - 1)

ADVECTION = 0.3
DIFFUSION = 0.1
MIXING = 0.1


def offset_of(slot):
    def far_first(a):
        return 2 - a + (a // 2) * (3 - 2 * (a % 2))

    return far_first(slot // 8), far_first((slot // 2) % 4), 1 - slot % 2


def peer_of(slot):
    me = lax.axis_index("gx")
    dy, dx, dc = offset_of(slot)
    y = (me // 8 + dy) % 4
    x = ((me // 2) % 4 + dx) % 4
    return y * 8 + x * 2 + (me % 2 + dc) % 2


def kernel(
    p_ref, r_ref, we_ref, wn_ref, col_ref, cnt_ref, w_ref,
    h_ref, scal_ref,
    col_send, col_recv, w_recv, w_sum, w_field,
    ext, ext_u, ext_v, abuf,
    row_send, row_recv, edge_send, edge_recv,
    red_send, red_plane, red_mid, red_depth,
    w_ss, w_rs, own_sem, col_ss, col_rs, halo_ss, halo_rs, red_ss, red_rs,
):
    me = lax.axis_index("gx")
    gy = lax.axis_index("gy")
    south, north = (gy + DEPTH - 1) % DEPTH, (gy + 1) % DEPTH
    west, east = (me + PLANE - 1) % PLANE, (me + 1) % PLANE
    lane = lax.broadcasted_iota(jnp.int32, (ROWS, COLS), 1)
    even = lane % 2 == 0
    pair = lane // 2

    barrier = pltpu.get_barrier_semaphore()

    @pl.loop(0, PLANE - 1)
    def _(slot):
        pl.semaphore_signal(barrier, inc=1, device_id={"gx": peer_of(slot)}, device_id_type=MESH)

    @pl.loop(1, DEPTH)
    def _(dz):
        pl.semaphore_signal(barrier, inc=1, device_id={"gy": (gy + dz) % DEPTH}, device_id_type=MESH)

    own = pl.multiple_of(me * COLS, COLS)
    own_copy = pltpu.make_async_copy(w_ref.at[:, :, pl.ds(own, COLS)], w_recv.at[:, PLANE - 1], own_sem)
    own_copy.start()
    slot_id = lax.broadcasted_iota(jnp.int32, (STEPS, COLS), 1)
    counts = cnt_ref[...]
    for g in range(PLANE):
        live = slot_id < counts[:, g : g + 1]
        col_send[g, :STEPS, :] = jnp.where(live, col_ref[:, g * COLS : (g + 1) * COLS], -1)
    col_recv[PLANE - 1] = col_send[me]

    for t in range(STEPS + 1):
        ext[t, 0] = jnp.zeros((PITCH, COLS), F32)
        ext[t, LEVELS - 1] = jnp.zeros((PITCH, COLS), F32)
    for s in range(STEPS):
        abuf[s, 0] = jnp.zeros((ROWS, COLS), F32)
        abuf[s, LEVELS - 1] = jnp.zeros((ROWS, COLS), F32)

    def rolled_edges(field, l, acc):
        return jnp.where(pair == l, pltpu.roll(field, 2 * l + 1, 1), acc)

    def load_level(l, carry):
        edges, rr, pp = carry
        f = p_ref[l]
        r = r_ref[l]
        ext[0, l + 1, 8:16, :] = f
        return rolled_edges(f, l, edges), rr + r * r, pp + f * f

    zero = jnp.zeros((ROWS, COLS), F32)
    edges, rr_part, pp_part = lax.fori_loop(0, L, load_level, (zero, zero, zero), unroll=8)

    pl.semaphore_wait(barrier, PLANE - 1 + DEPTH - 1)

    def col_copy(slot):
        return pltpu.make_async_remote_copy(
            src_ref=col_send.at[peer_of(slot)], dst_ref=col_recv.at[slot],
            send_sem=col_ss.at[slot], recv_sem=col_rs.at[slot],
            device_id={"gx": peer_of(slot)}, device_id_type=MESH,
        )

    def weight_copy(order, slot):
        p = peer_of(slot)
        return pltpu.make_async_remote_copy(
            src_ref=w_ref.at[STEPS - 1 - order, :, pl.ds(pl.multiple_of(p * COLS, COLS), COLS)],
            dst_ref=w_recv.at[STEPS - 1 - order, slot],
            send_sem=w_ss.at[order, slot], recv_sem=w_rs.at[order, slot],
            device_id={"gx": p}, device_id_type=MESH,
        )

    def send_weights(first, count):
        @pl.loop(first, first + count)
        def _(i):
            weight_copy(i // (PLANE - 1), i % (PLANE - 1)).start()

    def halo_copies(k):
        to = ({"gy": south}, {"gy": north}, {"gx": west}, {"gx": east})
        src = (row_send.at[k, 0], row_send.at[k, 1], edge_send.at[k], edge_send.at[k])
        dst = (row_recv.at[k, 1], row_recv.at[k, 0], edge_recv.at[k, 1], edge_recv.at[k, 0])
        return [
            pltpu.make_async_remote_copy(
                src_ref=src[i], dst_ref=dst[i], send_sem=halo_ss.at[k, i], recv_sem=halo_rs.at[k, i],
                device_id=to[i], device_id_type=MESH,
            )
            for i in range(4)
        ]

    def flat(ref, index):
        return ref.at[index].reshape(LEVELS * PITCH, COLS)

    def send_halo(k, low, high, edges):
        row_send[k, 0] = low[pl.ds(PITCH + 8, L, stride=PITCH), :]
        row_send[k, 1] = high[pl.ds(PITCH + 15, L, stride=PITCH), :]
        edge_send[k] = edges
        for copy in halo_copies(k):
            copy.start()

    def take_halo(k, low, high):
        for copy in halo_copies(k):
            copy.wait_recv()
        low[pl.ds(PITCH + 7, L, stride=PITCH), :] = jnp.where(gy > 0, row_recv[k, 0], 0.0)
        high[pl.ds(PITCH + 16, L, stride=PITCH), :] = jnp.where(gy < DEPTH - 1, row_recv[k, 1], 0.0)
        from_west = jnp.where(me > 0, edge_recv[k, 0], 0.0)
        from_east = jnp.where(me < PLANE - 1, edge_recv[k, 1], 0.0)
        return jnp.where(even, pltpu.roll(from_east, COLS - 1, 1), pltpu.roll(from_west, 1, 1))

    for t in range(1, STEPS + 1):
        state = flat(ext, t - 1)
        send_halo(t - 1, state, state, edges)
        if t == 1:
            @pl.loop(0, PLANE - 1)
            def _(slot):
                col_copy(slot).start()
        send_weights((t - 1) * OPENING, OPENING)
        beside = take_halo(t - 1, state, state)

        def tangent_level(l, edges, t=t, beside=beside):
            f = ext[t - 1, l + 1, 8:16, :]
            up = ext[t - 1, l + 1, 9:17, :]
            down = ext[t - 1, l + 1, 7:15, :]
            border = pltpu.roll(beside, COLS - 1 - 2 * l, 1)
            right = jnp.where(lane == COLS - 1, border, pltpu.roll(f, COLS - 1, 1))
            left = jnp.where(lane == 0, border, pltpu.roll(f, 1, 1))
            levels = ext[t - 1, l + 2, 8:16, :] + ext[t - 1, l, 8:16, :]
            out = (
                f
                - ADVECTION * (we_ref[l] * (right - left) + wn_ref[l] * (up - down))
                + DIFFUSION * (up + down + right + left - 4.0 * f)
                + MIXING * (levels - 2.0 * f)
            )
            ext[t, l + 1, 8:16, :] = out
            return rolled_edges(out, l, edges)

        edges = lax.fori_loop(0, L, tangent_level, zero, unroll=8)

    own_copy.wait()

    @pl.loop(0, PLANE - 1)
    def _(slot):
        col_copy(slot).wait_recv()

    cell = lax.broadcasted_iota(jnp.int32, (2 * COLS, GROUP * COLS), 0)

    def add_group(t, group, first):
        weights = jnp.concatenate([w_recv[t, group * GROUP + j] for j in range(GROUP)], axis=1)
        ids = jnp.concatenate([col_recv[group * GROUP + j, t : t + 1, :] for j in range(GROUP)], axis=1)
        high = weights.astype(jnp.bfloat16)
        low = (weights - high.astype(F32)).astype(jnp.bfloat16)
        both = jnp.concatenate([high, low], axis=0)
        for q in range(CELLS // (2 * COLS)):
            chosen = jnp.where(cell == ids - q * 2 * COLS, 1.0, 0.0).astype(jnp.bfloat16)
            part = lax.dot_general(both, chosen, (((1,), (1,)), ((), ())), preferred_element_type=F32)
            here = pl.ds(q * 2 * COLS, 2 * COLS)
            w_sum[:, here] = part if first else w_sum[:, here] + part

    def sum_weights(order):
        t = STEPS - 1 - order

        def one(group, first):
            for j in range(GROUP):
                weight_copy(order, group * GROUP + j).wait_recv()
            number = order * (CHUNKS - 1) + group
            start = STEPS * OPENING + number * GROUP

            @pl.when(start < SENDS)
            def _():
                send_weights(start, GROUP)

            add_group(t, group, first)

        one(0, True)

        @pl.loop(1, CHUNKS - 1)
        def _(group):
            one(group, False)

        for j in range(GROUP - 1):
            weight_copy(order, (CHUNKS - 1) * GROUP + j).wait_recv()
        add_group(t, CHUNKS - 1, False)
        field = w_field.reshape(L * ROWS, COLS)
        for r in range(ROWS):
            here = pl.ds(r * COLS, COLS)
            field[pl.ds(r, L, stride=ROWS), :] = w_sum[:L, here] + w_sum[L:, here]

    def adjoint_of(s, l, beside):
        a = abuf[s, l + 1]
        border = pltpu.roll(beside, COLS - 1 - 2 * l, 1)
        we = ADVECTION * we_ref[l]
        right = jnp.where(lane == COLS - 1, border, pltpu.roll((DIFFUSION + we) * a, COLS - 1, 1))
        left = jnp.where(lane == 0, border, pltpu.roll((DIFFUSION - we) * a, 1, 1))
        up = ext_u[s, l + 1, 9:17, :]
        down = ext_v[s, l + 1, 7:15, :]
        centre = 1.0 - 4.0 * DIFFUSION - 2.0 * MIXING
        return centre * a + (right + left) + (up + down) + MIXING * (abuf[s, l + 2] + abuf[s, l])

    pq_part = pp_part
    beside = None
    for order in range(STEPS):
        sum_weights(order)
        if order:
            beside = take_halo(STEPS + order - 1, flat(ext_v, order - 1), flat(ext_u, order - 1))

        def adjoint_level(l, carry, order=order, beside=beside):
            edges, pq = carry
            state = ext[STEPS - order, l + 1, 8:16, :]
            forcing = w_field[l] * state
            a = forcing + adjoint_of(order - 1, l, beside) if order else forcing
            we = ADVECTION * we_ref[l]
            wn = ADVECTION * wn_ref[l]
            abuf[order, l + 1] = a
            ext_u[order, l + 1, 8:16, :] = (DIFFUSION + wn) * a
            ext_v[order, l + 1, 8:16, :] = (DIFFUSION - wn) * a
            sent = jnp.where(lane == COLS - 1, DIFFUSION - we, DIFFUSION + we) * a
            return rolled_edges(sent, l, edges), pq + forcing * state

        edges, pq_part = lax.fori_loop(0, L, adjoint_level, (zero, pq_part), unroll=8)
        send_halo(STEPS + order, flat(ext_u, order), flat(ext_v, order), edges)

    def plane_copy(k, slot):
        return pltpu.make_async_remote_copy(
            src_ref=red_send.at[k], dst_ref=red_plane.at[k, slot],
            send_sem=red_ss.at[k, slot], recv_sem=red_rs.at[k, slot],
            device_id={"gx": peer_of(slot)}, device_id_type=MESH,
        )

    def depth_copy(k, dz):
        return pltpu.make_async_remote_copy(
            src_ref=red_mid.at[k], dst_ref=red_depth.at[k, dz - 1],
            send_sem=red_ss.at[k, PLANE - 1 + dz], recv_sem=red_rs.at[k, PLANE - 1 + dz],
            device_id={"gy": (gy + dz) % DEPTH}, device_id_type=MESH,
        )

    def reduce_start(k, value):
        red_send[k] = value

        @pl.loop(0, PLANE - 1)
        def _(slot):
            plane_copy(k, slot).start()

    def reduce_finish(k):
        @pl.loop(0, PLANE - 1)
        def _(slot):
            plane_copy(k, slot).wait_recv()

        total = red_send[k]
        for slot in range(PLANE - 1):
            total = total + red_plane[k, slot]
        red_mid[k] = total
        for dz in range(1, DEPTH):
            depth_copy(k, dz).start()
        for dz in range(1, DEPTH):
            depth_copy(k, dz).wait_recv()
        for dz in range(1, DEPTH):
            total = total + red_depth[k, dz - 1]
        return total

    row = lax.broadcasted_iota(jnp.int32, (ROWS, COLS), 0)
    upper = row < ROWS // 2
    rr_half = rr_part + pltpu.roll(rr_part, ROWS // 2, 0)
    pq_half = pq_part + pltpu.roll(pq_part, ROWS // 2, 0)
    reduce_start(0, jnp.where(upper, rr_half, pq_half))
    beside = take_halo(2 * STEPS - 1, flat(ext_v, STEPS - 1), flat(ext_u, STEPS - 1))

    def hessian_level(l, carry):
        h_ref[l] = p_ref[l] + adjoint_of(STEPS - 1, l, beside)
        return carry

    lax.fori_loop(0, L, hessian_level, 0, unroll=8)
    both = reduce_finish(0)
    rr = jnp.sum(jnp.where(upper, both, 0.0), axis=(0, 1), keepdims=True)
    pq = jnp.sum(jnp.where(upper, 0.0, both), axis=(0, 1), keepdims=True)
    alpha = jnp.broadcast_to(rr / pq, (ROWS, COLS))

    def residual_level(l, total):
        new = r_ref[l] - alpha * h_ref[l]
        return total + new * new

    reduce_start(1, lax.fori_loop(0, L, residual_level, zero, unroll=8))
    rr_next = jnp.sum(reduce_finish(1), axis=(0, 1), keepdims=True)
    scal_ref[0] = alpha
    scal_ref[1] = jnp.broadcast_to(rr_next / rr, (ROWS, COLS))

    for k in range(2 * STEPS):
        for copy in halo_copies(k):
            copy.wait_send()

    @pl.loop(0, PLANE - 1)
    def _(slot):
        col_copy(slot).wait_send()
        for order in range(STEPS):
            weight_copy(order, slot).wait_send()
        for k in range(2):
            plane_copy(k, slot).wait_send()

    for k in range(2):
        for dz in range(1, DEPTH):
            depth_copy(k, dz).wait_send()


def shards(increment, residual, direction, wind_east, wind_north, obs_column, obs_count, obs_weight):
    vmem = pl.BlockSpec(memory_space=pltpu.VMEM)
    dma = pltpu.SemaphoreType.DMA
    hessian, scalars = pl.pallas_call(
        kernel,
        out_shape=(
            jax.ShapeDtypeStruct((L, ROWS, COLS), F32),
            jax.ShapeDtypeStruct((2, ROWS, COLS), F32),
        ),
        in_specs=[vmem] * 6 + [pl.BlockSpec(memory_space=pl.ANY)],
        out_specs=(vmem, vmem),
        scratch_shapes=[
            pltpu.VMEM((PLANE, 8, COLS), jnp.int32),
            pltpu.VMEM((PLANE, 8, COLS), jnp.int32),
            pltpu.VMEM((STEPS, PLANE, L, COLS), F32),
            pltpu.VMEM((2 * L, CELLS), F32),
            pltpu.VMEM((L, ROWS, COLS), F32),
            pltpu.VMEM((STEPS + 1, LEVELS, PITCH, COLS), F32),
            pltpu.VMEM((STEPS, LEVELS, PITCH, COLS), F32),
            pltpu.VMEM((STEPS, LEVELS, PITCH, COLS), F32),
            pltpu.VMEM((STEPS, LEVELS, ROWS, COLS), F32),
            pltpu.VMEM((2 * STEPS, 2, L, COLS), F32),
            pltpu.VMEM((2 * STEPS, 2, L, COLS), F32),
            pltpu.VMEM((2 * STEPS, ROWS, COLS), F32),
            pltpu.VMEM((2 * STEPS, 2, ROWS, COLS), F32),
            pltpu.VMEM((2, ROWS, COLS), F32),
            pltpu.VMEM((2, PLANE - 1, ROWS, COLS), F32),
            pltpu.VMEM((2, ROWS, COLS), F32),
            pltpu.VMEM((2, DEPTH - 1, ROWS, COLS), F32),
            dma((STEPS, PLANE)), dma((STEPS, PLANE)), dma, dma((PLANE,)), dma((PLANE,)),
            dma((2 * STEPS, 4)), dma((2 * STEPS, 4)),
            dma((2, PLANE + DEPTH)), dma((2, PLANE + DEPTH)),
        ],
        compiler_params=pltpu.CompilerParams(
            collective_id=0, has_side_effects=True, vmem_limit_bytes=40 * 2**20
        ),
    )(direction, residual, wind_east, wind_north, obs_column, obs_count, obs_weight)
    alpha = scalars[0, 0, 0]
    beta = scalars[1, 0, 0]
    new_increment = increment + alpha * direction
    new_residual = residual - alpha * hessian
    new_direction = new_residual + beta * direction
    return new_increment, new_residual, new_direction


def solution(mesh):
    field = P(None, "gy", "gx")
    slots = P(None, ("gy", "gx"))
    return jax.shard_map(
        shards,
        mesh=mesh,
        in_specs=(field, field, field, field, field, slots, slots, P(None, None, ("gy", "gx"))),
        out_specs=(field, field, field),
        check_vma=False,
    )
```

```python
import functools

import jax
import jax.numpy as jnp
from jax import lax
from jax.experimental import pallas as pl
from jax.experimental.pallas import tpu as pltpu
from jax.sharding import PartitionSpec as P

MESH = pl.DeviceIdType.MESH
F32 = jnp.float32
STEPS = 4
L = 64
ROWS = 8
COLS = 128
CELLS = ROWS * COLS
PLANE = 32
DEPTH = 8
PITCH = 24
LEVELS = L + 2
GROUP = 4
CHUNKS = PLANE // GROUP
OPENING = 10
SENDS = STEPS * (PLANE - 1)

ADVECTION = 0.3
DIFFUSION = 0.1
MIXING = 0.1
SMALL = 2.0**-32


def offset_of(slot):
    def far_first(a):
        return 2 - a + (a // 2) * (3 - 2 * (a % 2))

    return far_first(slot // 8), far_first((slot // 2) % 4), 1 - slot % 2


def peer_of(slot):
    me = lax.axis_index("gx")
    dy, dx, dc = offset_of(slot)
    y = (me // 8 + dy) % 4
    x = ((me // 2) % 4 + dx) % 4
    return y * 8 + x * 2 + (me % 2 + dc) % 2


def two_sum(a, b):
    s = a + b
    t = s - a
    return s, (a - (s - t)) + (b - t)


def halves(a):
    c = 4097.0 * a
    high = c - (c - a)
    return high, a - high


def two_product(a, b):
    p = a * b
    ah, al = halves(a)
    bh, bl = halves(b)
    return p, ((ah * bh - p) + ah * bl + al * bh) + al * bl


def add_product(total, a, b):
    high, low = total
    p, rest = two_product(a, b)
    high, lost = two_sum(high, p)
    return high, low + (lost + rest)


def fold_rows(total):
    high, low = total
    for shift in (4, 2, 1):
        high, lost = two_sum(high, pltpu.roll(high, shift, 0))
        low = low + pltpu.roll(low, shift, 0) + lost
    return high, low


def kernel(
    p_hbm, r_hbm, we_hbm, wn_hbm, col_hbm, cnt_hbm, w_hbm,
    h_ref, alpha_ref, beta_ref,
    p_ref, r_ref, we_ref, wn_ref, col_ref, cnt_ref,
    w_send, w_recv, w_sum, w_field,
    ext, ext_u, ext_v, abuf,
    row_send, row_recv, edge_send, edge_recv,
    red_send, red_plane, red_mid, red_depth,
    in_sem, block_sem, w_ss, w_rs, halo_ss, halo_rs, red_ss, red_rs,
):
    me = lax.axis_index("gx")
    gy = lax.axis_index("gy")
    south, north = (gy + DEPTH - 1) % DEPTH, (gy + 1) % DEPTH
    west, east = (me + PLANE - 1) % PLANE, (me + 1) % PLANE
    lane = lax.broadcasted_iota(jnp.int32, (ROWS, COLS), 1)
    even = lane % 2 == 0
    pair = lane // 2

    loads = [
        pltpu.make_async_copy(src, dst, in_sem.at[i])
        for i, (src, dst) in enumerate((
            (cnt_hbm, cnt_ref), (col_hbm, col_ref), (p_hbm, p_ref),
            (r_hbm, r_ref), (we_hbm, we_ref), (wn_hbm, wn_ref),
        ))
    ]
    for load in loads:
        load.start()

    def block_load(g):
        here = pl.ds(pl.multiple_of(g * COLS, COLS), COLS)
        return pltpu.make_async_copy(w_hbm.at[:, :, here], w_send.at[:, g, pl.ds(0, L)], block_sem.at[g])

    @pl.loop(0, PLANE)
    def _(g):
        block_load(g).start()

    barrier = pltpu.get_barrier_semaphore()

    @pl.loop(0, PLANE - 1)
    def _(slot):
        pl.semaphore_signal(barrier, inc=1, device_id={"gx": peer_of(slot)}, device_id_type=MESH)

    @pl.loop(1, DEPTH)
    def _(dz):
        pl.semaphore_signal(barrier, inc=1, device_id={"gy": (gy + dz) % DEPTH}, device_id_type=MESH)

    loads[0].wait()
    loads[1].wait()
    slot_id = lax.broadcasted_iota(jnp.int32, (STEPS, COLS), 1)
    counts = cnt_ref[...]
    for g in range(PLANE):
        live = slot_id < counts[:, g : g + 1]
        columns = jnp.where(live, col_ref[:, g * COLS : (g + 1) * COLS], -1).astype(F32)
        w_send[STEPS - 1, g, L : L + STEPS, :] = columns
        w_send[STEPS - 1, g, L + STEPS :, :] = columns

    for t in range(STEPS + 1):
        ext[t, 0] = jnp.zeros((PITCH, COLS), F32)
        ext[t, LEVELS - 1] = jnp.zeros((PITCH, COLS), F32)
    for s in range(STEPS):
        abuf[s, 0] = jnp.zeros((ROWS, COLS), F32)
        abuf[s, LEVELS - 1] = jnp.zeros((ROWS, COLS), F32)

    for load in loads[2:]:
        load.wait()

    def rolled_edges(field, l, acc):
        return jnp.where(pair == l, pltpu.roll(field, 2 * l + 1, 1), acc)

    def load_level(l, carry):
        edges, rr, pp = carry
        f = p_ref[l]
        r = r_ref[l]
        ext[0, l + 1, 8:16, :] = f
        return rolled_edges(f, l, edges), add_product(rr, r, r), pp + f * f

    zero = jnp.zeros((ROWS, COLS), F32)
    edges, rr_part, pp_part = lax.fori_loop(0, L, load_level, (zero, (zero, zero), zero), unroll=8)

    @pl.loop(0, PLANE)
    def _(g):
        block_load(g).wait()

    pl.semaphore_wait(barrier, PLANE - 1 + DEPTH - 1)

    def weight_copy(order, slot, height):
        p = peer_of(slot)
        t = STEPS - 1 - order
        return pltpu.make_async_remote_copy(
            src_ref=w_send.at[t, p, pl.ds(0, height)],
            dst_ref=w_recv.at[t, slot, pl.ds(0, height)],
            send_sem=w_ss.at[order, slot], recv_sem=w_rs.at[order, slot],
            device_id={"gx": p}, device_id_type=MESH,
        )

    def height_of(order):
        return L if order else L + ROWS

    def send_weights(first, count):
        @pl.loop(first, first + count)
        def _(i):
            order, slot = i // (PLANE - 1), i % (PLANE - 1)

            @pl.when(order == 0)
            def _():
                weight_copy(0, slot, L + ROWS).start()

            @pl.when(order > 0)
            def _():
                weight_copy(order, slot, L).start()

    def halo_copies(k):
        to = ({"gy": south}, {"gy": north}, {"gx": west}, {"gx": east})
        src = (row_send.at[k, 0], row_send.at[k, 1], edge_send.at[k], edge_send.at[k])
        dst = (row_recv.at[k, 1], row_recv.at[k, 0], edge_recv.at[k, 1], edge_recv.at[k, 0])
        return [
            pltpu.make_async_remote_copy(
                src_ref=src[i], dst_ref=dst[i], send_sem=halo_ss.at[k, i], recv_sem=halo_rs.at[k, i],
                device_id=to[i], device_id_type=MESH,
            )
            for i in range(4)
        ]

    def flat(ref, index):
        return ref.at[index].reshape(LEVELS * PITCH, COLS)

    def send_halo(k, low, high, edges):
        row_send[k, 0] = low[pl.ds(PITCH + 8, L, stride=PITCH), :]
        row_send[k, 1] = high[pl.ds(PITCH + 15, L, stride=PITCH), :]
        edge_send[k] = edges
        for copy in halo_copies(k):
            copy.start()

    def take_halo(k, low, high):
        for copy in halo_copies(k):
            copy.wait_recv()
        low[pl.ds(PITCH + 7, L, stride=PITCH), :] = jnp.where(gy > 0, row_recv[k, 0], 0.0)
        high[pl.ds(PITCH + 16, L, stride=PITCH), :] = jnp.where(gy < DEPTH - 1, row_recv[k, 1], 0.0)
        from_west = jnp.where(me > 0, edge_recv[k, 0], 0.0)
        from_east = jnp.where(me < PLANE - 1, edge_recv[k, 1], 0.0)
        return jnp.where(even, pltpu.roll(from_east, COLS - 1, 1), pltpu.roll(from_west, 1, 1))

    for t in range(1, STEPS + 1):
        state = flat(ext, t - 1)
        send_halo(t - 1, state, state, edges)
        send_weights((t - 1) * OPENING, OPENING)
        beside = take_halo(t - 1, state, state)

        def tangent_level(l, edges, t=t, beside=beside):
            f = ext[t - 1, l + 1, 8:16, :]
            up = ext[t - 1, l + 1, 9:17, :]
            down = ext[t - 1, l + 1, 7:15, :]
            border = pltpu.roll(beside, COLS - 1 - 2 * l, 1)
            right = jnp.where(lane == COLS - 1, border, pltpu.roll(f, COLS - 1, 1))
            left = jnp.where(lane == 0, border, pltpu.roll(f, 1, 1))
            levels = ext[t - 1, l + 2, 8:16, :] + ext[t - 1, l, 8:16, :]
            out = (
                f
                - ADVECTION * (we_ref[l] * (right - left) + wn_ref[l] * (up - down))
                + DIFFUSION * (up + down + right + left - 4.0 * f)
                + MIXING * (levels - 2.0 * f)
            )
            ext[t, l + 1, 8:16, :] = out
            return rolled_edges(out, l, edges)

        edges = lax.fori_loop(0, L, tangent_level, zero, unroll=8)

    cell = lax.broadcasted_iota(jnp.int32, (2 * COLS, GROUP * COLS), 0).astype(F32)

    def add_group(t, group, own, first):
        slots = [group * GROUP + j for j in range(GROUP)]
        blocks = [w_recv.at[t, slot] for slot in slots]
        columns = [w_recv.at[STEPS - 1, slot] for slot in slots]
        if own:
            blocks[-1], columns[-1] = w_send.at[t, me], w_send.at[STEPS - 1, me]
        weights = jnp.concatenate([block[:L, :] for block in blocks], axis=1)
        ids = jnp.concatenate([column[L + t : L + t + 1, :] for column in columns], axis=1)
        high = weights.astype(jnp.bfloat16)
        low = (weights - high.astype(F32)).astype(jnp.bfloat16)
        both = jnp.concatenate([high, low], axis=0)
        for q in range(CELLS // (2 * COLS)):
            chosen = jnp.where(cell == ids - float(q * 2 * COLS), 1.0, 0.0).astype(jnp.bfloat16)
            part = lax.dot_general(both, chosen, (((1,), (1,)), ((), ())), preferred_element_type=F32)
            here = pl.ds(q * 2 * COLS, 2 * COLS)
            w_sum[:, here] = part if first else w_sum[:, here] + part

    def sum_weights(order):
        t = STEPS - 1 - order

        def one(group, first):
            for j in range(GROUP):
                weight_copy(order, group * GROUP + j, height_of(order)).wait_recv()
            number = order * (CHUNKS - 1) + group
            start = STEPS * OPENING + number * GROUP

            @pl.when(start < SENDS)
            def _():
                send_weights(start, GROUP)

            add_group(t, group, False, first)

        one(0, True)

        @pl.loop(1, CHUNKS - 1)
        def _(group):
            one(group, False)

        for j in range(GROUP - 1):
            weight_copy(order, (CHUNKS - 1) * GROUP + j, height_of(order)).wait_recv()
        add_group(t, CHUNKS - 1, True, False)
        field = w_field.reshape(L * ROWS, COLS)
        for r in range(ROWS):
            here = pl.ds(r * COLS, COLS)
            field[pl.ds(r, L, stride=ROWS), :] = w_sum[:L, here] + w_sum[L:, here]

    def adjoint_of(s, l, beside):
        a = abuf[s, l + 1]
        border = pltpu.roll(beside, COLS - 1 - 2 * l, 1)
        we = ADVECTION * we_ref[l]
        right = jnp.where(lane == COLS - 1, border, pltpu.roll((DIFFUSION + we) * a, COLS - 1, 1))
        left = jnp.where(lane == 0, border, pltpu.roll((DIFFUSION - we) * a, 1, 1))
        up = ext_u[s, l + 1, 9:17, :]
        down = ext_v[s, l + 1, 7:15, :]
        centre = 1.0 - 4.0 * DIFFUSION - 2.0 * MIXING
        return centre * a + (right + left) + (up + down) + MIXING * (abuf[s, l + 2] + abuf[s, l])

    pq_part = pp_part
    beside = None
    for order in range(STEPS):
        sum_weights(order)
        if order:
            beside = take_halo(STEPS + order - 1, flat(ext_v, order - 1), flat(ext_u, order - 1))

        def adjoint_level(l, carry, order=order, beside=beside):
            edges, pq = carry
            state = ext[STEPS - order, l + 1, 8:16, :]
            forcing = w_field[l] * state
            a = forcing + adjoint_of(order - 1, l, beside) if order else forcing
            we = ADVECTION * we_ref[l]
            wn = ADVECTION * wn_ref[l]
            abuf[order, l + 1] = a
            ext_u[order, l + 1, 8:16, :] = (DIFFUSION + wn) * a
            ext_v[order, l + 1, 8:16, :] = (DIFFUSION - wn) * a
            sent = jnp.where(lane == COLS - 1, DIFFUSION - we, DIFFUSION + we) * a
            return rolled_edges(sent, l, edges), pq + forcing * state

        edges, pq_part = lax.fori_loop(0, L, adjoint_level, (zero, pq_part), unroll=8)
        send_halo(STEPS + order, flat(ext_u, order), flat(ext_v, order), edges)

    def plane_copy(slot):
        return pltpu.make_async_remote_copy(
            src_ref=red_send, dst_ref=red_plane.at[slot],
            send_sem=red_ss.at[slot], recv_sem=red_rs.at[slot],
            device_id={"gx": peer_of(slot)}, device_id_type=MESH,
        )

    def depth_copy(dz):
        return pltpu.make_async_remote_copy(
            src_ref=red_mid, dst_ref=red_depth.at[dz - 1],
            send_sem=red_ss.at[PLANE - 1 + dz], recv_sem=red_rs.at[PLANE - 1 + dz],
            device_id={"gy": (gy + dz) % DEPTH}, device_id_type=MESH,
        )

    row = lax.broadcasted_iota(jnp.int32, (ROWS, COLS), 0)
    upper = row < ROWS // 2

    def add(a, b):
        total, lost = two_sum(a[0], b[0])
        return jnp.where(upper, total, total + pltpu.roll(lost, ROWS // 2, 0)), a[1] + b[1]

    def add_all(terms):
        while len(terms) > 1:
            terms = [add(*terms[i : i + 2]) if i + 1 < len(terms) else terms[i] for i in range(0, len(terms), 2)]
        return terms[0]

    beside = take_halo(2 * STEPS - 1, flat(ext_v, STEPS - 1), flat(ext_u, STEPS - 1))

    def hessian_level(l, carry):
        rh, hh, rg, gg = carry
        h = p_ref[l] + adjoint_of(STEPS - 1, l, beside)
        r = r_ref[l]
        g = h * SMALL
        h_ref[l] = h
        return add_product(rh, r, h), add_product(hh, h, h), rg + r * g, gg + g * g

    rh, hh, rg, gg = lax.fori_loop(0, L, hessian_level, ((zero, zero), (zero, zero), zero, zero), unroll=8)
    rr_high, rr_low = fold_rows(rr_part)
    rh_high, rh_low = fold_rows(rh)
    hh_high, hh_low = fold_rows(hh)
    pq_high, pq_low = fold_rows((pq_part, zero))
    parts = (rr_high, rh_high, hh_high, pq_high, rr_low, rh_low, hh_low, pq_low)
    tile = zero
    for i, part in enumerate(parts):
        tile = jnp.where(row == i, part, tile)
    rg, _ = fold_rows((rg, zero))
    gg, _ = fold_rows((gg, zero))
    red_send[0] = tile
    red_send[1] = jnp.where(row == 0, rg, gg)

    @pl.loop(0, PLANE - 1)
    def _(slot):
        plane_copy(slot).start()

    @pl.loop(0, PLANE - 1)
    def _(slot):
        plane_copy(slot).wait_recv()

    total = add_all(
        [(red_send[0], red_send[1])] + [(red_plane[i, 0], red_plane[i, 1]) for i in range(PLANE - 1)]
    )
    red_mid[0] = total[0]
    red_mid[1] = total[1]
    for dz in range(1, DEPTH):
        depth_copy(dz).start()
    for dz in range(1, DEPTH):
        depth_copy(dz).wait_recv()
    total = add_all([total] + [(red_depth[i, 0], red_depth[i, 1]) for i in range(DEPTH - 1)])
    for shift in (64, 32, 16, 8, 4, 2, 1):
        total = add(total, (pltpu.roll(total[0], shift, 1), pltpu.roll(total[1], shift, 1)))

    def at(tile, i):
        return jnp.broadcast_to(tile[i : i + 1], (ROWS, COLS))

    rr_high, rr_low = two_sum(at(total[0], 0), at(total[0], 4))
    rh_high, rh_low = two_sum(at(total[0], 1), at(total[0], 5))
    hh_high, hh_low = two_sum(at(total[0], 2), at(total[0], 6))
    alpha = rr_high / (at(total[0], 3) + at(total[0], 7))
    high, low = two_product(alpha, hh_high)
    high, lost = two_sum(2.0 * rh_high, -high)
    low = lost + (2.0 * rh_low - (low + alpha * hh_low))
    high, low = two_sum(high, low)
    after, rest = two_product(alpha, high)
    after, lost = two_sum(rr_high, -after)
    rr_next = after + (lost + (rr_low - (rest + alpha * low)))
    rg, gg = at(total[1], 0), at(total[1], 1)
    scaled = alpha * (1.0 / SMALL)
    rr_far = rr_high - scaled * (2.0 * rg - scaled * gg)
    rr_next = jnp.where(gg < 1e10, rr_next, rr_far)
    alpha_ref[...] = alpha
    beta_ref[...] = rr_next / rr_high

    for k in range(2 * STEPS):
        for copy in halo_copies(k):
            copy.wait_send()

    @pl.loop(0, PLANE - 1)
    def _(slot):
        for order in range(STEPS):
            weight_copy(order, slot, height_of(order)).wait_send()
        plane_copy(slot).wait_send()

    for dz in range(1, DEPTH):
        depth_copy(dz).wait_send()


def shards(increment, residual, direction, wind_east, wind_north, obs_column, obs_count, obs_weight):
    vmem = pl.BlockSpec(memory_space=pltpu.VMEM)
    dma = pltpu.SemaphoreType.DMA
    any_space = pl.BlockSpec(memory_space=pl.ANY)
    hessian, alpha, beta = pl.pallas_call(
        kernel,
        out_shape=(
            jax.ShapeDtypeStruct((L, ROWS, COLS), F32),
            jax.ShapeDtypeStruct((ROWS, COLS), F32),
            jax.ShapeDtypeStruct((ROWS, COLS), F32),
        ),
        in_specs=[any_space] * 7,
        out_specs=(vmem, vmem, vmem),
        scratch_shapes=[
            pltpu.VMEM((L, ROWS, COLS), F32),
            pltpu.VMEM((L, ROWS, COLS), F32),
            pltpu.VMEM((L, ROWS, COLS), F32),
            pltpu.VMEM((L, ROWS, COLS), F32),
            pltpu.VMEM((STEPS, PLANE * COLS), jnp.int32),
            pltpu.VMEM((STEPS, PLANE), jnp.int32),
            pltpu.VMEM((STEPS, PLANE, L + ROWS, COLS), F32),
            pltpu.VMEM((STEPS, PLANE, L + ROWS, COLS), F32),
            pltpu.VMEM((2 * L, CELLS), F32),
            pltpu.VMEM((L, ROWS, COLS), F32),
            pltpu.VMEM((STEPS + 1, LEVELS, PITCH, COLS), F32),
            pltpu.VMEM((STEPS, LEVELS, PITCH, COLS), F32),
            pltpu.VMEM((STEPS, LEVELS, PITCH, COLS), F32),
            pltpu.VMEM((STEPS, LEVELS, ROWS, COLS), F32),
            pltpu.VMEM((2 * STEPS, 2, L, COLS), F32),
            pltpu.VMEM((2 * STEPS, 2, L, COLS), F32),
            pltpu.VMEM((2 * STEPS, ROWS, COLS), F32),
            pltpu.VMEM((2 * STEPS, 2, ROWS, COLS), F32),
            pltpu.VMEM((2, ROWS, COLS), F32),
            pltpu.VMEM((PLANE - 1, 2, ROWS, COLS), F32),
            pltpu.VMEM((2, ROWS, COLS), F32),
            pltpu.VMEM((DEPTH - 1, 2, ROWS, COLS), F32),
            dma((6,)), dma((PLANE,)), dma((STEPS, PLANE)), dma((STEPS, PLANE)),
            dma((2 * STEPS, 4)), dma((2 * STEPS, 4)),
            dma((PLANE + DEPTH,)), dma((PLANE + DEPTH,)),
        ],
        compiler_params=pltpu.CompilerParams(
            collective_id=0, has_side_effects=True, vmem_limit_bytes=60 * 2**20
        ),
    )(direction, residual, wind_east, wind_north, obs_column, obs_count, obs_weight)
    new_increment = increment + alpha * direction
    new_residual = residual - alpha * hessian
    new_direction = new_residual + beta * direction
    return new_increment, new_residual, new_direction


def solution(mesh):
    field = P(None, "gy", "gx")
    slots = P(None, ("gy", "gx"))
    return jax.shard_map(
        shards,
        mesh=mesh,
        in_specs=(field, field, field, field, field, slots, slots, P(None, None, ("gy", "gx"))),
        out_specs=(field, field, field),
        check_vma=False,
    )
```

```python
import functools

import jax
import jax.numpy as jnp
from jax import lax
from jax.experimental import pallas as pl
from jax.experimental.pallas import tpu as pltpu
from jax.sharding import PartitionSpec as P

MESH = pl.DeviceIdType.MESH
F32 = jnp.float32
STEPS = 4
L = 64
ROWS = 8
COLS = 128
CELLS = ROWS * COLS
PLANE = 32
DEPTH = 8
PITCH = 24
LEVELS = L + 2
GROUP = 4
CHUNKS = PLANE // GROUP
OPENING = 14
STRIDE = 13
SENDS = STEPS * (PLANE - 1)

ADVECTION = 0.3
DIFFUSION = 0.1
MIXING = 0.1
SMALL = 2.0**-32


def offset_of(slot):
    o = STRIDE * (PLANE - 1 - slot) % PLANE
    return o // 8, (o // 2) % 4, o % 2


def peer_of(slot):
    me = lax.axis_index("gx")
    dy, dx, dc = offset_of(slot)
    y = (me // 8 + dy) % 4
    x = ((me // 2) % 4 + dx) % 4
    return y * 8 + x * 2 + (me % 2 + dc) % 2


def two_sum(a, b):
    s = a + b
    t = s - a
    return s, (a - (s - t)) + (b - t)


def halves(a):
    c = 4097.0 * a
    high = c - (c - a)
    return high, a - high


def two_product(a, b):
    p = a * b
    ah, al = halves(a)
    bh, bl = halves(b)
    return p, ((ah * bh - p) + ah * bl + al * bh) + al * bl


def add_product(total, a, b):
    high, low = total
    p, rest = two_product(a, b)
    high, lost = two_sum(high, p)
    return high, low + (lost + rest)


def fold_rows(total):
    high, low = total
    for shift in (4, 2, 1):
        high, lost = two_sum(high, pltpu.roll(high, shift, 0))
        low = low + pltpu.roll(low, shift, 0) + lost
    return high, low


def kernel(
    p_hbm, r_hbm, we_hbm, wn_hbm, col_hbm, cnt_hbm, w_hbm,
    h_ref, alpha_ref, beta_ref,
    p_ref, r_ref, we_ref, wn_ref, col_ref, cnt_ref,
    w_send, w_recv, w_sum, w_field,
    ext, ext_u, ext_v, abuf,
    row_send, row_recv, edge_send, edge_recv,
    red_send, red_plane, red_mid, red_depth,
    in_sem, block_sem, w_ss, w_rs, halo_ss, halo_rs, red_ss, red_rs,
):
    me = lax.axis_index("gx")
    gy = lax.axis_index("gy")
    south, north = (gy + DEPTH - 1) % DEPTH, (gy + 1) % DEPTH
    west, east = (me + PLANE - 1) % PLANE, (me + 1) % PLANE
    lane = lax.broadcasted_iota(jnp.int32, (ROWS, COLS), 1)
    even = lane % 2 == 0
    pair = lane // 2

    loads = [
        pltpu.make_async_copy(src, dst, in_sem.at[i])
        for i, (src, dst) in enumerate((
            (cnt_hbm, cnt_ref), (col_hbm, col_ref), (p_hbm, p_ref),
            (r_hbm, r_ref), (we_hbm, we_ref), (wn_hbm, wn_ref),
        ))
    ]
    weight_loads = [
        pltpu.make_async_copy(w_hbm.at[t], w_send.at[t, pl.ds(0, L)], block_sem.at[t]) for t in range(STEPS)
    ]
    for load in loads[:3] + weight_loads[::-1] + loads[3:]:
        load.start()

    barrier = pltpu.get_barrier_semaphore()

    for slot in range(PLANE - 1):
        pl.semaphore_signal(barrier, inc=1, device_id={"gx": peer_of(slot)}, device_id_type=MESH)

    for dz in range(1, DEPTH):
        pl.semaphore_signal(barrier, inc=1, device_id={"gy": (gy + dz) % DEPTH}, device_id_type=MESH)

    loads[0].wait()
    loads[1].wait()
    slot_id = lax.broadcasted_iota(jnp.int32, (STEPS, COLS), 1)
    counts = cnt_ref[...]
    for g in range(PLANE):
        live = slot_id < counts[:, g : g + 1]
        columns = jnp.where(live, col_ref[:, g * COLS : (g + 1) * COLS], -1).astype(F32)
        here = slice(g * COLS, (g + 1) * COLS)
        w_send[STEPS - 1, L : L + STEPS, here] = columns
        w_send[STEPS - 1, L + STEPS :, here] = columns

    for t in range(STEPS + 1):
        ext[t, 0] = jnp.zeros((PITCH, COLS), F32)
        ext[t, LEVELS - 1] = jnp.zeros((PITCH, COLS), F32)
    for s in range(STEPS):
        abuf[s, 0] = jnp.zeros((ROWS, COLS), F32)
        abuf[s, LEVELS - 1] = jnp.zeros((ROWS, COLS), F32)

    loads[2].wait()

    def rolled_edges(field, l, acc):
        return jnp.where(pair == l, pltpu.roll(field, 2 * l + 1, 1), acc)

    def load_level(l, carry):
        edges, pp = carry
        f = p_ref[l]
        ext[0, l + 1, 8:16, :] = f
        return rolled_edges(f, l, edges), pp + f * f

    zero = jnp.zeros((ROWS, COLS), F32)
    edges, pp_part = lax.fori_loop(0, L, load_level, (zero, zero), unroll=8)

    weight_loads[STEPS - 1].wait()
    pl.semaphore_wait(barrier, PLANE - 1 + DEPTH - 1)

    def weight_copy(order, slot, height):
        p = peer_of(slot)
        t = STEPS - 1 - order
        return pltpu.make_async_remote_copy(
            src_ref=w_send.at[t, pl.ds(0, height), pl.ds(pl.multiple_of(p * COLS, COLS), COLS)],
            dst_ref=w_recv.at[t, slot, pl.ds(0, height)],
            send_sem=w_ss.at[order, slot], recv_sem=w_rs.at[order, slot],
            device_id={"gx": p}, device_id_type=MESH,
        )

    def height_of(order):
        return L if order else L + ROWS

    def send_weights(first, count):
        @pl.loop(first, first + count)
        def _(i):
            order, slot = i // (PLANE - 1), i % (PLANE - 1)

            @pl.when(order == 0)
            def _():
                weight_copy(0, slot, L + ROWS).start()

            @pl.when(order > 0)
            def _():
                weight_copy(order, slot, L).start()

    def halo_copies(k):
        to = ({"gy": south}, {"gy": north}, {"gx": west}, {"gx": east})
        src = (row_send.at[k, 0], row_send.at[k, 1], edge_send.at[k], edge_send.at[k])
        dst = (row_recv.at[k, 1], row_recv.at[k, 0], edge_recv.at[k, 1], edge_recv.at[k, 0])
        return [
            pltpu.make_async_remote_copy(
                src_ref=src[i], dst_ref=dst[i], send_sem=halo_ss.at[k, i], recv_sem=halo_rs.at[k, i],
                device_id=to[i], device_id_type=MESH,
            )
            for i in range(4)
        ]

    def flat(ref, index):
        return ref.at[index].reshape(LEVELS * PITCH, COLS)

    def send_halo(k, low, high, edges):
        row_send[k, 0] = low[pl.ds(PITCH + 8, L, stride=PITCH), :]
        row_send[k, 1] = high[pl.ds(PITCH + 15, L, stride=PITCH), :]
        edge_send[k] = edges
        for copy in halo_copies(k):
            copy.start()

    def take_halo(k, low, high):
        for copy in halo_copies(k):
            copy.wait_recv()
        low[pl.ds(PITCH + 7, L, stride=PITCH), :] = jnp.where(gy > 0, row_recv[k, 0], 0.0)
        high[pl.ds(PITCH + 16, L, stride=PITCH), :] = jnp.where(gy < DEPTH - 1, row_recv[k, 1], 0.0)
        from_west = jnp.where(me > 0, edge_recv[k, 0], 0.0)
        from_east = jnp.where(me < PLANE - 1, edge_recv[k, 1], 0.0)
        return jnp.where(even, pltpu.roll(from_east, COLS - 1, 1), pltpu.roll(from_west, 1, 1))

    for t in range(1, STEPS + 1):
        state = flat(ext, t - 1)
        send_halo(t - 1, state, state, edges)
        send_weights((t - 1) * OPENING, OPENING)
        if t == 1:
            for load in loads[3:] + weight_loads[: STEPS - 1]:
                load.wait()
            rr_part = lax.fori_loop(
                0, L, lambda l, rr: add_product(rr, r_ref[l], r_ref[l]), (zero, zero), unroll=8
            )
        beside = take_halo(t - 1, state, state)

        def tangent_level(l, edges, t=t, beside=beside):
            f = ext[t - 1, l + 1, 8:16, :]
            up = ext[t - 1, l + 1, 9:17, :]
            down = ext[t - 1, l + 1, 7:15, :]
            border = pltpu.roll(beside, COLS - 1 - 2 * l, 1)
            right = jnp.where(lane == COLS - 1, border, pltpu.roll(f, COLS - 1, 1))
            left = jnp.where(lane == 0, border, pltpu.roll(f, 1, 1))
            levels = ext[t - 1, l + 2, 8:16, :] + ext[t - 1, l, 8:16, :]
            out = (
                f
                - ADVECTION * (we_ref[l] * (right - left) + wn_ref[l] * (up - down))
                + DIFFUSION * (up + down + right + left - 4.0 * f)
                + MIXING * (levels - 2.0 * f)
            )
            ext[t, l + 1, 8:16, :] = out
            return rolled_edges(out, l, edges)

        edges = lax.fori_loop(0, L, tangent_level, zero, unroll=8)

    cell = lax.broadcasted_iota(jnp.int32, (2 * COLS, GROUP * COLS), 0).astype(F32)

    def add_group(t, group, own, first):
        slots = [group * GROUP + j for j in range(GROUP)]
        blocks = [w_recv.at[t, slot] for slot in slots]
        columns = [w_recv.at[STEPS - 1, slot] for slot in slots]
        if own:
            mine = pl.ds(pl.multiple_of(me * COLS, COLS), COLS)
            blocks[-1], columns[-1] = w_send.at[t, :, mine], w_send.at[STEPS - 1, :, mine]
        weights = jnp.concatenate([block[:L, :] for block in blocks], axis=1)
        ids = jnp.concatenate([column[L + t : L + t + 1, :] for column in columns], axis=1)
        high = weights.astype(jnp.bfloat16)
        low = (weights - high.astype(F32)).astype(jnp.bfloat16)
        both = jnp.concatenate([high, low], axis=0)
        for q in range(CELLS // (2 * COLS)):
            chosen = jnp.where(cell == ids - float(q * 2 * COLS), 1.0, 0.0).astype(jnp.bfloat16)
            part = lax.dot_general(both, chosen, (((1,), (1,)), ((), ())), preferred_element_type=F32)
            here = pl.ds(q * 2 * COLS, 2 * COLS)
            w_sum[:, here] = part if first else w_sum[:, here] + part

    def sum_weights(order):
        t = STEPS - 1 - order

        def one(group, first):
            for j in range(GROUP):
                weight_copy(order, group * GROUP + j, height_of(order)).wait_recv()
            number = order * (CHUNKS - 1) + group
            start = STEPS * OPENING + number * GROUP

            @pl.when(start < SENDS)
            def _():
                send_weights(start, GROUP)

            add_group(t, group, False, first)

        one(0, True)

        @pl.loop(1, CHUNKS - 1)
        def _(group):
            one(group, False)

        for j in range(GROUP - 1):
            weight_copy(order, (CHUNKS - 1) * GROUP + j, height_of(order)).wait_recv()
        add_group(t, CHUNKS - 1, True, False)
        field = w_field.reshape(L * ROWS, COLS)
        for r in range(ROWS):
            here = pl.ds(r * COLS, COLS)
            field[pl.ds(r, L, stride=ROWS), :] = w_sum[:L, here] + w_sum[L:, here]

    def adjoint_of(s, l, beside):
        a = abuf[s, l + 1]
        border = pltpu.roll(beside, COLS - 1 - 2 * l, 1)
        we = ADVECTION * we_ref[l]
        right = jnp.where(lane == COLS - 1, border, pltpu.roll((DIFFUSION + we) * a, COLS - 1, 1))
        left = jnp.where(lane == 0, border, pltpu.roll((DIFFUSION - we) * a, 1, 1))
        up = ext_u[s, l + 1, 9:17, :]
        down = ext_v[s, l + 1, 7:15, :]
        centre = 1.0 - 4.0 * DIFFUSION - 2.0 * MIXING
        return centre * a + (right + left) + (up + down) + MIXING * (abuf[s, l + 2] + abuf[s, l])

    pq_part = pp_part
    beside = None
    for order in range(STEPS):
        sum_weights(order)
        if order:
            beside = take_halo(STEPS + order - 1, flat(ext_v, order - 1), flat(ext_u, order - 1))

        def adjoint_level(l, carry, order=order, beside=beside):
            edges, pq = carry
            state = ext[STEPS - order, l + 1, 8:16, :]
            forcing = w_field[l] * state
            a = forcing + adjoint_of(order - 1, l, beside) if order else forcing
            we = ADVECTION * we_ref[l]
            wn = ADVECTION * wn_ref[l]
            abuf[order, l + 1] = a
            ext_u[order, l + 1, 8:16, :] = (DIFFUSION + wn) * a
            ext_v[order, l + 1, 8:16, :] = (DIFFUSION - wn) * a
            sent = jnp.where(lane == COLS - 1, DIFFUSION - we, DIFFUSION + we) * a
            return rolled_edges(sent, l, edges), pq + forcing * state

        edges, pq_part = lax.fori_loop(0, L, adjoint_level, (zero, pq_part), unroll=8)
        send_halo(STEPS + order, flat(ext_u, order), flat(ext_v, order), edges)

    def plane_copy(slot):
        return pltpu.make_async_remote_copy(
            src_ref=red_send, dst_ref=red_plane.at[slot],
            send_sem=red_ss.at[slot], recv_sem=red_rs.at[slot],
            device_id={"gx": peer_of(slot)}, device_id_type=MESH,
        )

    def depth_copy(dz):
        return pltpu.make_async_remote_copy(
            src_ref=red_mid, dst_ref=red_depth.at[dz - 1],
            send_sem=red_ss.at[PLANE - 1 + dz], recv_sem=red_rs.at[PLANE - 1 + dz],
            device_id={"gy": (gy + dz) % DEPTH}, device_id_type=MESH,
        )

    row = lax.broadcasted_iota(jnp.int32, (ROWS, COLS), 0)
    upper = row < ROWS // 2

    def add(a, b):
        total, lost = two_sum(a, b)
        return jnp.where(upper, total, total + pltpu.roll(lost, ROWS // 2, 0))

    def add_all(terms):
        while len(terms) > 1:
            terms = [add(*terms[i : i + 2]) if i + 1 < len(terms) else terms[i] for i in range(0, len(terms), 2)]
        return terms[0]

    beside = take_halo(2 * STEPS - 1, flat(ext_v, STEPS - 1), flat(ext_u, STEPS - 1))

    def hessian_level(l, carry):
        rh, hh, rg, gg = carry
        h = p_ref[l] + adjoint_of(STEPS - 1, l, beside)
        r = r_ref[l]
        g = h * SMALL
        h_ref[l] = h
        return add_product(rh, r, h), add_product(hh, h, h), rg + r * g, gg + g * g

    rh, hh, rg, gg = lax.fori_loop(0, L, hessian_level, ((zero, zero), (zero, zero), zero, zero), unroll=8)
    rr_high, rr_low = fold_rows(rr_part)
    rh_high, rh_low = fold_rows(rh)
    hh_high, hh_low = fold_rows(hh)
    pq_high, pq_low = fold_rows((pq_part, zero))
    parts = (rr_high, rh_high, hh_high, pq_high, rr_low, rh_low, hh_low, pq_low)
    tile = zero
    for i, part in enumerate(parts):
        tile = jnp.where(row == i, part, tile)
    rg, _ = fold_rows((rg, zero))
    gg, _ = fold_rows((gg, zero))
    far = jnp.where(row == 0, rg, jnp.where(row == 1, gg, 0.0))
    half = COLS // 2
    tile = add(tile, pltpu.roll(tile, half, 1))
    far = add(far, pltpu.roll(far, half, 1))
    red_send[...] = jnp.where(lane < half, tile, far)

    for slot in range(PLANE - 1):
        plane_copy(slot).start()
    for slot in range(PLANE - 1):
        plane_copy(slot).wait_recv()

    total = add_all([red_send[...]] + [red_plane[i] for i in range(PLANE - 1)])
    red_mid[...] = total
    for dz in range(1, DEPTH):
        depth_copy(dz).start()
    for dz in range(1, DEPTH):
        depth_copy(dz).wait_recv()
    total = add_all([total] + [red_depth[i] for i in range(DEPTH - 1)])
    for shift in (32, 16, 8, 4, 2, 1):
        total = add(total, pltpu.roll(total, COLS - shift, 1))

    def at(i, first=0):
        return jnp.broadcast_to(total[i : i + 1, first : first + 1], (ROWS, COLS))

    rr_high, rr_low = two_sum(at(0), at(4))
    rh_high, rh_low = two_sum(at(1), at(5))
    hh_high, hh_low = two_sum(at(2), at(6))
    alpha = rr_high / (at(3) + at(7))
    high, low = two_product(alpha, hh_high)
    high, lost = two_sum(2.0 * rh_high, -high)
    low = lost + (2.0 * rh_low - (low + alpha * hh_low))
    high, low = two_sum(high, low)
    after, rest = two_product(alpha, high)
    after, lost = two_sum(rr_high, -after)
    rr_next = after + (lost + (rr_low - (rest + alpha * low)))
    rg, gg = at(0, half), at(1, half)
    scaled = alpha * (1.0 / SMALL)
    rr_far = rr_high - scaled * (2.0 * rg - scaled * gg)
    rr_next = jnp.where(gg < 1e10, rr_next, rr_far)
    alpha_ref[...] = alpha
    beta_ref[...] = rr_next / rr_high

    for k in range(2 * STEPS):
        for copy in halo_copies(k):
            copy.wait_send()

    @pl.loop(0, PLANE - 1)
    def _(slot):
        for order in range(STEPS):
            weight_copy(order, slot, height_of(order)).wait_send()
        plane_copy(slot).wait_send()

    for dz in range(1, DEPTH):
        depth_copy(dz).wait_send()


def shards(increment, residual, direction, wind_east, wind_north, obs_column, obs_count, obs_weight):
    vmem = pl.BlockSpec(memory_space=pltpu.VMEM)
    dma = pltpu.SemaphoreType.DMA
    any_space = pl.BlockSpec(memory_space=pl.ANY)
    hessian, alpha, beta = pl.pallas_call(
        kernel,
        out_shape=(
            jax.ShapeDtypeStruct((L, ROWS, COLS), F32),
            jax.ShapeDtypeStruct((ROWS, COLS), F32),
            jax.ShapeDtypeStruct((ROWS, COLS), F32),
        ),
        in_specs=[any_space] * 7,
        out_specs=(vmem, vmem, vmem),
        scratch_shapes=[
            pltpu.VMEM((L, ROWS, COLS), F32),
            pltpu.VMEM((L, ROWS, COLS), F32),
            pltpu.VMEM((L, ROWS, COLS), F32),
            pltpu.VMEM((L, ROWS, COLS), F32),
            pltpu.VMEM((STEPS, PLANE * COLS), jnp.int32),
            pltpu.VMEM((STEPS, PLANE), jnp.int32),
            pltpu.VMEM((STEPS, L + ROWS, PLANE * COLS), F32),
            pltpu.VMEM((STEPS, PLANE, L + ROWS, COLS), F32),
            pltpu.VMEM((2 * L, CELLS), F32),
            pltpu.VMEM((L, ROWS, COLS), F32),
            pltpu.VMEM((STEPS + 1, LEVELS, PITCH, COLS), F32),
            pltpu.VMEM((STEPS, LEVELS, PITCH, COLS), F32),
            pltpu.VMEM((STEPS, LEVELS, PITCH, COLS), F32),
            pltpu.VMEM((STEPS, LEVELS, ROWS, COLS), F32),
            pltpu.VMEM((2 * STEPS, 2, L, COLS), F32),
            pltpu.VMEM((2 * STEPS, 2, L, COLS), F32),
            pltpu.VMEM((2 * STEPS, ROWS, COLS), F32),
            pltpu.VMEM((2 * STEPS, 2, ROWS, COLS), F32),
            pltpu.VMEM((ROWS, COLS), F32),
            pltpu.VMEM((PLANE - 1, ROWS, COLS), F32),
            pltpu.VMEM((ROWS, COLS), F32),
            pltpu.VMEM((DEPTH - 1, ROWS, COLS), F32),
            dma((6,)), dma((STEPS,)), dma((STEPS, PLANE)), dma((STEPS, PLANE)),
            dma((2 * STEPS, 4)), dma((2 * STEPS, 4)),
            dma((PLANE + DEPTH,)), dma((PLANE + DEPTH,)),
        ],
        compiler_params=pltpu.CompilerParams(
            collective_id=0, has_side_effects=True, vmem_limit_bytes=60 * 2**20
        ),
    )(direction, residual, wind_east, wind_north, obs_column, obs_count, obs_weight)
    new_increment = increment + alpha * direction
    new_residual = residual - alpha * hessian
    new_direction = new_residual + beta * direction
    return new_increment, new_residual, new_direction


def solution(mesh):
    field = P(None, "gy", "gx")
    slots = P(None, ("gy", "gx"))
    return jax.shard_map(
        shards,
        mesh=mesh,
        in_specs=(field, field, field, field, field, slots, slots, P(None, None, ("gy", "gx"))),
        out_specs=(field, field, field),
        check_vma=False,
    )
```

```python
import functools

import jax
import jax.numpy as jnp
from jax import lax
from jax.experimental import pallas as pl
from jax.experimental.pallas import tpu as pltpu
from jax.sharding import PartitionSpec as P

MESH = pl.DeviceIdType.MESH
F32 = jnp.float32
STEPS = 4
L = 64
ROWS = 8
COLS = 128
CELLS = ROWS * COLS
PLANE = 32
DEPTH = 8
PITCH = 24
LEVELS = L + 2
GROUP = 4
CHUNKS = PLANE // GROUP
OPENING = 14
STRIDE = 13
SENDS = STEPS * (PLANE - 1)

ADVECTION = 0.3
DIFFUSION = 0.1
MIXING = 0.1
SMALL = 2.0**-32


def offset_of(slot):
    o = STRIDE * (PLANE - 1 - slot) % PLANE
    return o // 8, (o // 2) % 4, o % 2


def peer_of(slot):
    me = lax.axis_index("gx")
    dy, dx, dc = offset_of(slot)
    y = (me // 8 + dy) % 4
    x = ((me // 2) % 4 + dx) % 4
    return y * 8 + x * 2 + (me % 2 + dc) % 2


def two_sum(a, b):
    s = a + b
    t = s - a
    return s, (a - (s - t)) + (b - t)


def halves(a):
    c = 4097.0 * a
    high = c - (c - a)
    return high, a - high


def two_product(a, b):
    p = a * b
    ah, al = halves(a)
    bh, bl = halves(b)
    return p, ((ah * bh - p) + ah * bl + al * bh) + al * bl


def add_product(total, a, b):
    high, low = total
    p, rest = two_product(a, b)
    high, lost = two_sum(high, p)
    return high, low + (lost + rest)


def fold_rows(total):
    high, low = total
    for shift in (4, 2, 1):
        high, lost = two_sum(high, pltpu.roll(high, shift, 0))
        low = low + pltpu.roll(low, shift, 0) + lost
    return high, low


def kernel(
    p_hbm, r_hbm, we_hbm, wn_hbm, col_hbm, cnt_hbm, w_hbm,
    h_ref, alpha_ref, beta_ref,
    p_ref, r_ref, we_ref, wn_ref, col_ref, cnt_ref,
    w_send, w_recv, w_sum, w_field,
    ext, ext_u, ext_v, abuf,
    row_send, row_recv, edge_send, edge_recv,
    red_send, red_plane, red_mid, red_depth,
    in_sem, block_sem, w_ss, w_rs, halo_ss, halo_rs, red_ss, red_rs,
):
    me = lax.axis_index("gx")
    gy = lax.axis_index("gy")
    south, north = (gy + DEPTH - 1) % DEPTH, (gy + 1) % DEPTH
    west, east = (me + PLANE - 1) % PLANE, (me + 1) % PLANE
    lane = lax.broadcasted_iota(jnp.int32, (ROWS, COLS), 1)
    even = lane % 2 == 0
    pair = lane // 2

    loads = [
        pltpu.make_async_copy(src, dst, in_sem.at[i])
        for i, (src, dst) in enumerate((
            (cnt_hbm, cnt_ref), (col_hbm, col_ref), (p_hbm, p_ref),
            (r_hbm, r_ref), (we_hbm, we_ref), (wn_hbm, wn_ref),
        ))
    ]
    weight_loads = [
        pltpu.make_async_copy(w_hbm.at[t], w_send.at[t, pl.ds(0, L)], block_sem.at[t]) for t in range(STEPS)
    ]
    for load in loads[:3] + weight_loads[::-1] + loads[3:]:
        load.start()

    barrier = pltpu.get_barrier_semaphore()

    for slot in range(PLANE - 1):
        pl.semaphore_signal(barrier, inc=1, device_id={"gx": peer_of(slot)}, device_id_type=MESH)

    for dz in range(1, DEPTH):
        pl.semaphore_signal(barrier, inc=1, device_id={"gy": (gy + dz) % DEPTH}, device_id_type=MESH)

    loads[0].wait()
    loads[1].wait()
    slot_id = lax.broadcasted_iota(jnp.int32, (STEPS, COLS), 1)
    counts = cnt_ref[...]
    for g in range(PLANE):
        live = slot_id < counts[:, g : g + 1]
        columns = jnp.where(live, col_ref[:, g * COLS : (g + 1) * COLS], -1).astype(F32)
        here = slice(g * COLS, (g + 1) * COLS)
        w_send[STEPS - 1, L : L + STEPS, here] = columns
        w_send[STEPS - 1, L + STEPS :, here] = columns

    for t in range(STEPS + 1):
        ext[t, 0] = jnp.zeros((PITCH, COLS), F32)
        ext[t, LEVELS - 1] = jnp.zeros((PITCH, COLS), F32)
    for s in range(STEPS):
        abuf[s, 0] = jnp.zeros((ROWS, COLS), F32)
        abuf[s, LEVELS - 1] = jnp.zeros((ROWS, COLS), F32)

    loads[2].wait()

    def rolled_edges(field, l, acc):
        return jnp.where(pair == l, pltpu.roll(field, 2 * l + 1, 1), acc)

    def load_level(l, carry):
        edges, pp = carry
        f = p_ref[l]
        ext[0, l + 1, 8:16, :] = f
        return rolled_edges(f, l, edges), pp + f * f

    zero = jnp.zeros((ROWS, COLS), F32)
    edges, pp_part = lax.fori_loop(0, L, load_level, (zero, zero), unroll=8)

    weight_loads[STEPS - 1].wait()
    pl.semaphore_wait(barrier, PLANE - 1 + DEPTH - 1)

    def weight_copy(order, slot, height):
        p = peer_of(slot)
        t = STEPS - 1 - order
        return pltpu.make_async_remote_copy(
            src_ref=w_send.at[t, pl.ds(0, height), pl.ds(pl.multiple_of(p * COLS, COLS), COLS)],
            dst_ref=w_recv.at[t, slot, pl.ds(0, height)],
            send_sem=w_ss.at[order, slot], recv_sem=w_rs.at[order, slot],
            device_id={"gx": p}, device_id_type=MESH,
        )

    def height_of(order):
        return L if order else L + ROWS

    def send_weights(first, count):
        @pl.loop(first, first + count)
        def _(i):
            order, slot = i // (PLANE - 1), i % (PLANE - 1)

            @pl.when(order == 0)
            def _():
                weight_copy(0, slot, L + ROWS).start()

            @pl.when(order > 0)
            def _():
                weight_copy(order, slot, L).start()

    def halo_copies(k):
        to = ({"gy": south}, {"gy": north}, {"gx": west}, {"gx": east})
        src = (row_send.at[k, 0], row_send.at[k, 1], edge_send.at[k], edge_send.at[k])
        dst = (row_recv.at[k, 1], row_recv.at[k, 0], edge_recv.at[k, 1], edge_recv.at[k, 0])
        return [
            pltpu.make_async_remote_copy(
                src_ref=src[i], dst_ref=dst[i], send_sem=halo_ss.at[k, i], recv_sem=halo_rs.at[k, i],
                device_id=to[i], device_id_type=MESH,
            )
            for i in range(4)
        ]

    def flat(ref, index):
        return ref.at[index].reshape(LEVELS * PITCH, COLS)

    def send_halo(k, low, high, edges):
        row_send[k, 0] = low[pl.ds(PITCH + 8, L, stride=PITCH), :]
        row_send[k, 1] = high[pl.ds(PITCH + 15, L, stride=PITCH), :]
        edge_send[k] = edges
        for copy in halo_copies(k):
            copy.start()

    def take_halo(k, low, high):
        for copy in halo_copies(k):
            copy.wait_recv()
        low[pl.ds(PITCH + 7, L, stride=PITCH), :] = jnp.where(gy > 0, row_recv[k, 0], 0.0)
        high[pl.ds(PITCH + 16, L, stride=PITCH), :] = jnp.where(gy < DEPTH - 1, row_recv[k, 1], 0.0)
        from_west = jnp.where(me > 0, edge_recv[k, 0], 0.0)
        from_east = jnp.where(me < PLANE - 1, edge_recv[k, 1], 0.0)
        return jnp.where(even, pltpu.roll(from_east, COLS - 1, 1), pltpu.roll(from_west, 1, 1))

    for t in range(1, STEPS + 1):
        state = flat(ext, t - 1)
        send_halo(t - 1, state, state, edges)
        send_weights((t - 1) * OPENING, OPENING)
        if t == 1:
            for load in loads[3:] + weight_loads[: STEPS - 1]:
                load.wait()
            rr_part = lax.fori_loop(
                0, L, lambda l, rr: add_product(rr, r_ref[l], r_ref[l]), (zero, zero), unroll=8
            )
        beside = take_halo(t - 1, state, state)

        def tangent_level(l, edges, t=t, beside=beside):
            f = ext[t - 1, l + 1, 8:16, :]
            up = ext[t - 1, l + 1, 9:17, :]
            down = ext[t - 1, l + 1, 7:15, :]
            border = pltpu.roll(beside, COLS - 1 - 2 * l, 1)
            right = jnp.where(lane == COLS - 1, border, pltpu.roll(f, COLS - 1, 1))
            left = jnp.where(lane == 0, border, pltpu.roll(f, 1, 1))
            levels = ext[t - 1, l + 2, 8:16, :] + ext[t - 1, l, 8:16, :]
            out = (
                f
                - ADVECTION * (we_ref[l] * (right - left) + wn_ref[l] * (up - down))
                + DIFFUSION * (up + down + right + left - 4.0 * f)
                + MIXING * (levels - 2.0 * f)
            )
            ext[t, l + 1, 8:16, :] = out
            return rolled_edges(out, l, edges)

        edges = lax.fori_loop(0, L, tangent_level, zero, unroll=8)

    cell = lax.broadcasted_iota(jnp.int32, (2 * COLS, GROUP * COLS), 0).astype(F32)

    def add_group(t, group, own, first):
        slots = [group * GROUP + j for j in range(GROUP)]
        blocks = [w_recv.at[t, slot] for slot in slots]
        columns = [w_recv.at[STEPS - 1, slot] for slot in slots]
        if own:
            mine = pl.ds(pl.multiple_of(me * COLS, COLS), COLS)
            blocks[-1], columns[-1] = w_send.at[t, :, mine], w_send.at[STEPS - 1, :, mine]
        weights = jnp.concatenate([block[:L, :] for block in blocks], axis=1)
        ids = jnp.concatenate([column[L + t : L + t + 1, :] for column in columns], axis=1)
        high = weights.astype(jnp.bfloat16)
        low = (weights - high.astype(F32)).astype(jnp.bfloat16)
        both = jnp.concatenate([high, low], axis=0)
        for q in range(CELLS // (2 * COLS)):
            chosen = jnp.where(cell == ids - float(q * 2 * COLS), 1.0, 0.0).astype(jnp.bfloat16)
            part = lax.dot_general(both, chosen, (((1,), (1,)), ((), ())), preferred_element_type=F32)
            here = pl.ds(q * 2 * COLS, 2 * COLS)
            w_sum[:, here] = part if first else w_sum[:, here] + part

    def sum_weights(order):
        t = STEPS - 1 - order

        def one(group, first):
            for j in range(GROUP):
                weight_copy(order, group * GROUP + j, height_of(order)).wait_recv()
            number = order * (CHUNKS - 1) + group
            start = STEPS * OPENING + number * GROUP

            @pl.when(start < SENDS)
            def _():
                send_weights(start, GROUP)

            add_group(t, group, False, first)

        one(0, True)

        @pl.loop(1, CHUNKS - 1)
        def _(group):
            one(group, False)

        for j in range(GROUP - 1):
            weight_copy(order, (CHUNKS - 1) * GROUP + j, height_of(order)).wait_recv()
        add_group(t, CHUNKS - 1, True, False)
        field = w_field.reshape(L * ROWS, COLS)
        for r in range(ROWS):
            here = pl.ds(r * COLS, COLS)
            field[pl.ds(r, L, stride=ROWS), :] = w_sum[:L, here] + w_sum[L:, here]

    def adjoint_of(s, l, beside):
        a = abuf[s, l + 1]
        border = pltpu.roll(beside, COLS - 1 - 2 * l, 1)
        we = ADVECTION * we_ref[l]
        right = jnp.where(lane == COLS - 1, border, pltpu.roll((DIFFUSION + we) * a, COLS - 1, 1))
        left = jnp.where(lane == 0, border, pltpu.roll((DIFFUSION - we) * a, 1, 1))
        up = ext_u[s, l + 1, 9:17, :]
        down = ext_v[s, l + 1, 7:15, :]
        centre = 1.0 - 4.0 * DIFFUSION - 2.0 * MIXING
        return centre * a + (right + left) + (up + down) + MIXING * (abuf[s, l + 2] + abuf[s, l])

    pq_part = pp_part
    beside = None
    for order in range(STEPS):
        sum_weights(order)
        if order:
            beside = take_halo(STEPS + order - 1, flat(ext_v, order - 1), flat(ext_u, order - 1))

        def adjoint_level(l, carry, order=order, beside=beside):
            edges, pq = carry
            state = ext[STEPS - order, l + 1, 8:16, :]
            forcing = w_field[l] * state
            a = forcing + adjoint_of(order - 1, l, beside) if order else forcing
            we = ADVECTION * we_ref[l]
            wn = ADVECTION * wn_ref[l]
            abuf[order, l + 1] = a
            ext_u[order, l + 1, 8:16, :] = (DIFFUSION + wn) * a
            ext_v[order, l + 1, 8:16, :] = (DIFFUSION - wn) * a
            sent = jnp.where(lane == COLS - 1, DIFFUSION - we, DIFFUSION + we) * a
            return rolled_edges(sent, l, edges), pq + forcing * state

        edges, pq_part = lax.fori_loop(0, L, adjoint_level, (zero, pq_part), unroll=8)
        send_halo(STEPS + order, flat(ext_u, order), flat(ext_v, order), edges)

    def plane_copy(slot):
        return pltpu.make_async_remote_copy(
            src_ref=red_send, dst_ref=red_plane.at[slot],
            send_sem=red_ss.at[slot], recv_sem=red_rs.at[slot],
            device_id={"gx": peer_of(slot)}, device_id_type=MESH,
        )

    def depth_copy(dz):
        return pltpu.make_async_remote_copy(
            src_ref=red_mid, dst_ref=red_depth.at[dz - 1],
            send_sem=red_ss.at[PLANE - 1 + dz], recv_sem=red_rs.at[PLANE - 1 + dz],
            device_id={"gy": (gy + dz) % DEPTH}, device_id_type=MESH,
        )

    row = lax.broadcasted_iota(jnp.int32, (ROWS, COLS), 0)
    upper = row < ROWS // 2

    def add(a, b):
        total, lost = two_sum(a, b)
        return jnp.where(upper, total, total + pltpu.roll(lost, ROWS // 2, 0))

    def add_all(terms):
        while len(terms) > 1:
            terms = [add(*terms[i : i + 2]) if i + 1 < len(terms) else terms[i] for i in range(0, len(terms), 2)]
        return terms[0]

    beside = take_halo(2 * STEPS - 1, flat(ext_v, STEPS - 1), flat(ext_u, STEPS - 1))

    def hessian_level(l, carry):
        rh, hh, rg, gg = carry
        h = p_ref[l] + adjoint_of(STEPS - 1, l, beside)
        r = r_ref[l]
        g = h * SMALL
        h_ref[l] = h
        return add_product(rh, r, h), add_product(hh, h, h), rg + r * g, gg + g * g

    rh, hh, rg, gg = lax.fori_loop(0, L, hessian_level, ((zero, zero), (zero, zero), zero, zero), unroll=8)
    rr_high, rr_low = fold_rows(rr_part)
    rh_high, rh_low = fold_rows(rh)
    hh_high, hh_low = fold_rows(hh)
    pq_high, pq_low = fold_rows((pq_part, zero))
    parts = (rr_high, rh_high, hh_high, pq_high, rr_low, rh_low, hh_low, pq_low)
    tile = zero
    for i, part in enumerate(parts):
        tile = jnp.where(row == i, part, tile)
    rg, _ = fold_rows((rg, zero))
    gg, _ = fold_rows((gg, zero))
    far = jnp.where(row == 0, rg, jnp.where(row == 1, gg, 0.0))
    half = COLS // 2
    tile = add(tile, pltpu.roll(tile, half, 1))
    far = add(far, pltpu.roll(far, half, 1))
    red_send[...] = jnp.where(lane < half, tile, far)

    for slot in range(PLANE - 1):
        plane_copy(slot).start()
    for k in range(2 * STEPS):
        for copy in halo_copies(k):
            copy.wait_send()

    @pl.loop(0, PLANE - 1)
    def _(slot):
        for order in range(STEPS):
            weight_copy(order, slot, height_of(order)).wait_send()

    for slot in range(PLANE - 1):
        plane_copy(slot).wait_recv()

    total = add_all([red_send[...]] + [red_plane[i] for i in range(PLANE - 1)])
    red_mid[...] = total
    for dz in range(1, DEPTH):
        depth_copy(dz).start()
    for slot in range(PLANE - 1):
        plane_copy(slot).wait_send()
    for dz in range(1, DEPTH):
        depth_copy(dz).wait_recv()
    total = add_all([total] + [red_depth[i] for i in range(DEPTH - 1)])
    for shift in (32, 16, 8, 4, 2, 1):
        total = add(total, pltpu.roll(total, COLS - shift, 1))

    def at(i, first=0):
        return jnp.broadcast_to(total[i : i + 1, first : first + 1], (ROWS, COLS))

    rr_high, rr_low = two_sum(at(0), at(4))
    rh_high, rh_low = two_sum(at(1), at(5))
    hh_high, hh_low = two_sum(at(2), at(6))
    alpha = rr_high / (at(3) + at(7))
    high, low = two_product(alpha, hh_high)
    high, lost = two_sum(2.0 * rh_high, -high)
    low = lost + (2.0 * rh_low - (low + alpha * hh_low))
    high, low = two_sum(high, low)
    after, rest = two_product(alpha, high)
    after, lost = two_sum(rr_high, -after)
    rr_next = after + (lost + (rr_low - (rest + alpha * low)))
    rg, gg = at(0, half), at(1, half)
    scaled = alpha * (1.0 / SMALL)
    rr_far = rr_high - scaled * (2.0 * rg - scaled * gg)
    rr_next = jnp.where(gg < 1e10, rr_next, rr_far)
    alpha_ref[...] = alpha
    beta_ref[...] = rr_next / rr_high

    for dz in range(1, DEPTH):
        depth_copy(dz).wait_send()


def shards(increment, residual, direction, wind_east, wind_north, obs_column, obs_count, obs_weight):
    vmem = pl.BlockSpec(memory_space=pltpu.VMEM)
    dma = pltpu.SemaphoreType.DMA
    any_space = pl.BlockSpec(memory_space=pl.ANY)
    hessian, alpha, beta = pl.pallas_call(
        kernel,
        out_shape=(
            jax.ShapeDtypeStruct((L, ROWS, COLS), F32),
            jax.ShapeDtypeStruct((ROWS, COLS), F32),
            jax.ShapeDtypeStruct((ROWS, COLS), F32),
        ),
        in_specs=[any_space] * 7,
        out_specs=(vmem, vmem, vmem),
        scratch_shapes=[
            pltpu.VMEM((L, ROWS, COLS), F32),
            pltpu.VMEM((L, ROWS, COLS), F32),
            pltpu.VMEM((L, ROWS, COLS), F32),
            pltpu.VMEM((L, ROWS, COLS), F32),
            pltpu.VMEM((STEPS, PLANE * COLS), jnp.int32),
            pltpu.VMEM((STEPS, PLANE), jnp.int32),
            pltpu.VMEM((STEPS, L + ROWS, PLANE * COLS), F32),
            pltpu.VMEM((STEPS, PLANE, L + ROWS, COLS), F32),
            pltpu.VMEM((2 * L, CELLS), F32),
            pltpu.VMEM((L, ROWS, COLS), F32),
            pltpu.VMEM((STEPS + 1, LEVELS, PITCH, COLS), F32),
            pltpu.VMEM((STEPS, LEVELS, PITCH, COLS), F32),
            pltpu.VMEM((STEPS, LEVELS, PITCH, COLS), F32),
            pltpu.VMEM((STEPS, LEVELS, ROWS, COLS), F32),
            pltpu.VMEM((2 * STEPS, 2, L, COLS), F32),
            pltpu.VMEM((2 * STEPS, 2, L, COLS), F32),
            pltpu.VMEM((2 * STEPS, ROWS, COLS), F32),
            pltpu.VMEM((2 * STEPS, 2, ROWS, COLS), F32),
            pltpu.VMEM((ROWS, COLS), F32),
            pltpu.VMEM((PLANE - 1, ROWS, COLS), F32),
            pltpu.VMEM((ROWS, COLS), F32),
            pltpu.VMEM((DEPTH - 1, ROWS, COLS), F32),
            dma((6,)), dma((STEPS,)), dma((STEPS, PLANE)), dma((STEPS, PLANE)),
            dma((2 * STEPS, 4)), dma((2 * STEPS, 4)),
            dma((PLANE + DEPTH,)), dma((PLANE + DEPTH,)),
        ],
        compiler_params=pltpu.CompilerParams(
            collective_id=0, has_side_effects=True, vmem_limit_bytes=60 * 2**20
        ),
    )(direction, residual, wind_east, wind_north, obs_column, obs_count, obs_weight)
    new_increment = increment + alpha * direction
    new_residual = residual - alpha * hessian
    new_direction = new_residual + beta * direction
    return new_increment, new_residual, new_direction


def solution(mesh):
    field = P(None, "gy", "gx")
    slots = P(None, ("gy", "gx"))
    return jax.shard_map(
        shards,
        mesh=mesh,
        in_specs=(field, field, field, field, field, slots, slots, P(None, None, ("gy", "gx"))),
        out_specs=(field, field, field),
        check_vma=False,
    )
```
